256 devices in a mesh: seq: 32 (over y_lo, z, core), dp: 8 (over y_hi, x).
Axes of the slice: x: 4, y: 4 (y_hi: 2, y_lo: 2; y = y_hi * 2 + y_lo), z: 8, core: 2. Of those that a mesh axis runs over, the one named last changes fastest.
Arguments:
- features: bfloat16 [131072, 512], P(('dp', 'seq')), parts along dimension 0, may hold values from -6 to 6
- conv_gain: float32 [512], replicated, may hold values from 0.1 to 1.9
- conv_weight: bfloat16 [5, 512, 1536], replicated, may hold values from -0.125 to 0.125
- conv_bias: float32 [1536], replicated, may hold values from -3 to 3
- tower_gain: float32 [1536], replicated, may hold values from 0.1 to 1.9
- query_weight: bfloat16 [1536, 1024], replicated, may hold values from -4 to 4
- key_weight: bfloat16 [1536, 128], replicated, may hold values from -4 to 4
- value_weight: bfloat16 [1536, 192], replicated, may hold values from -0.15625 to 0.15625
- out_gain: float32 [1536], replicated, may hold values from 0.1 to 1.9
Outputs:
- tower_out: float32 [65536, 1536], P(('dp', 'seq')), parts along dimension 0
The draws below stay inside these ranges and needn't reach their ends.
There are 8 independent parts, one for each index of `dp`. The reference program is written for one: setup_inputs(seed, part) draws one part's arguments, and reference() takes and returns one part's arrays. A program takes and returns all parts, laid end to end along the dimension named above; an argument that names none is the same for every part. Nothing has to cross between parts.
All inputs are finite; a program needn't handle non-finite values.
Results may differ from the reference program's by a relative error of at most 0.0067.
Values may be sent and summed in bfloat16 or wider, within the bound.
No kernel may reach another device: no remote copies, remote signals or barrier semaphores. Data moves between devices by JAX's collectives and lax.ppermute only.
A program may use at most 192 MiB of HBM per device.

```python
import math
import jax
import jax.numpy as jnp
from jax import lax

CIN = 512
D = 1536
HEADS = 8
KD = 128
VD = 192
WIDTH = 5
L = 8192
ROWS = 16384


def shared_base(key):
    return jnp.clip(jax.random.normal(key, (D, KD), jnp.float32), -4.0, 4.0)


def draw_key_weight(key, part):
    base = shared_base(key)
    return (base / math.sqrt(D)).astype(jnp.bfloat16)


def draw_query_weight(key, part):
    key = jax.random.fold_in(key, 5)
    first_key = jax.random.fold_in(key, 0)
    own = jnp.clip(jax.random.normal(first_key, (D, HEADS * KD), jnp.float32), -4.0, 4.0) / math.sqrt(D)
    return own.astype(jnp.bfloat16)


def steps_of(stream_key, extent, cuts, low, largest):
    level = 1.0
    for position, shards_of in cuts:
        steps = jax.random.uniform(jax.random.fold_in(jax.random.fold_in(stream_key, 6), position), (shards_of,), jnp.float32, low / len(cuts), largest / len(cuts))
        level = level * jnp.repeat(jnp.exp(steps), extent[position] // shards_of).reshape((-1,) + (1,) * (len(extent) - 1 - position))
    return level


def noise(key, dims, scale, most, cuts=(), dtype=jnp.bfloat16):
    loudness = steps_of(key, dims, cuts, -0.22, 0.18) if cuts else 1.0
    entries = jax.random.normal(key, dims, jnp.float32) * scale * loudness
    return jnp.minimum(jnp.maximum(entries, -most), most).astype(dtype)


def setup_inputs(seed: int = 0, part: int = 0) -> dict:
    key_of = jax.random.split(jax.random.key(seed), 10)
    part_keys = jax.random.split(jax.random.fold_in(key_of[9], part), 10)
    features = noise(part_keys[0], (ROWS, CIN), 1.0, 6.0, ((0, 32),))
    conv_gain = jnp.clip(1.0 + 0.18 * jax.random.normal(key_of[1], (CIN,), jnp.float32), 0.1, 1.9)
    conv_weight = noise(key_of[2], (WIDTH, CIN, D), (WIDTH * CIN) ** -0.5, 0.125)
    conv_bias = noise(key_of[3], (D,), 0.5, 3.0, (), jnp.float32)
    tower_gain = jnp.clip(1.0 + 0.18 * jax.random.normal(key_of[4], (D,), jnp.float32), 0.1, 1.9)
    query_weight = draw_query_weight(jax.random.fold_in(key_of[9], 71), part)
    key_weight = draw_key_weight(jax.random.fold_in(key_of[9], 71), part)
    value_weight = noise(key_of[7], (D, VD), D ** -0.5, 0.15625)
    out_gain = jnp.clip(1.0 + 0.18 * jax.random.normal(key_of[8], (D,), jnp.float32), 0.1, 1.9)
    return dict(features=features, conv_gain=conv_gain, conv_weight=conv_weight, conv_bias=conv_bias, tower_gain=tower_gain, query_weight=query_weight, key_weight=key_weight, value_weight=value_weight, out_gain=out_gain)


def norm_rows(values, gain):
    mean_sq = lax.optimization_barrier(jnp.mean(values * values, axis=-1, keepdims=True))
    return values * lax.rsqrt(mean_sq + 1e-06) * gain

def reference(features, conv_gain, conv_weight, conv_bias, tower_gain, query_weight, key_weight, value_weight, out_gain):
    activated = jax.nn.gelu(norm_rows(features.astype(jnp.float32), conv_gain), approximate=False).astype(jnp.bfloat16)
    reach = (WIDTH - 1) // 2
    padded = jnp.pad(activated, ((reach, reach), (0, 0)))
    convolved = jnp.zeros((ROWS, D), jnp.float32) + conv_bias
    for offset in range(WIDTH):
        convolved = convolved + jnp.dot(padded[offset:offset + ROWS], conv_weight[offset], preferred_element_type=jnp.float32)
    pooled = jnp.maximum(convolved[0::2], convolved[1::2]).astype(jnp.bfloat16)
    normed = norm_rows(pooled.astype(jnp.float32), tower_gain).astype(jnp.bfloat16)
    queries = jnp.dot(normed, query_weight, preferred_element_type=jnp.float32).astype(jnp.bfloat16)
    keys_all = jnp.dot(normed, key_weight, preferred_element_type=jnp.float32).astype(jnp.bfloat16)
    values_all = jnp.dot(normed, value_weight, preferred_element_type=jnp.float32).astype(jnp.bfloat16)
    score_scale = 1.0 / math.sqrt(KD)
    block_len = min(L, 512)
    query_blocks = queries.reshape(L // block_len, block_len * HEADS, KD)

    def attend_block(query_rows):
        scores = lax.dot_general(query_rows, keys_all, (((1,), (1,)), ((), ())), preferred_element_type=jnp.float32) * score_scale
        top_row = lax.optimization_barrier(jnp.max(scores, axis=1, keepdims=True))
        expon = jnp.exp(scores - top_row)
        total = lax.optimization_barrier(jnp.sum(expon, axis=1, keepdims=True))
        mixed = jnp.dot(expon.astype(jnp.bfloat16), values_all, preferred_element_type=jnp.float32)
        return mixed / total
    attended = lax.map(attend_block, query_blocks).reshape(L, HEADS * VD)
    return norm_rows(attended, out_gain)
```

```python
import functools
import math

import jax
import jax.numpy as jnp
from jax import lax
from jax.experimental import pallas as pl
from jax.experimental.pallas import tpu as pltpu
from jax.sharding import PartitionSpec as P

F32 = jnp.float32
BF16 = jnp.bfloat16
EPS = 1e-06
MIB = 2**20
SHIFT = 32.0
BIG = 2.0**100
VMEM = pl.BlockSpec(memory_space=pltpu.VMEM)
HBM = pl.BlockSpec(memory_space=pltpu.HBM)


def norm_gelu(rows, gain):
    mean_sq = jnp.mean(rows * rows, axis=-1, keepdims=True)
    normed = rows * lax.rsqrt(mean_sq + EPS) * gain
    return 0.5 * normed * (1.0 + lax.erf(normed * math.sqrt(0.5)))


def activate_kernel(feat_ref, gain_ref, weight_ref, taps_ref, lead_ref, feat, gain, scr, sems):
    copies = [
        pltpu.make_async_copy(feat_ref, feat, sems.at[0]),
        pltpu.make_async_copy(gain_ref, gain, sems.at[1]),
    ]
    cin = feat.shape[1]
    for tap in range(lead_ref.shape[0] // cin):
        copies.append(
            pltpu.make_async_copy(
                weight_ref.at[tap], lead_ref.at[pl.ds(tap * cin, cin)], sems.at[2 + tap]
            )
        )
    for copy in copies:
        copy.start()
    for copy in copies[:2]:
        copy.wait()
    rows, cin = feat.shape
    half = rows // 2
    scr_cols = scr.shape[2]
    active = norm_gelu(feat[...].astype(F32), gain[...])
    place = lax.broadcasted_iota(jnp.int32, (half, scr_cols), 0)
    for i in range(scr.shape[0]):
        scr[i] = active[:, i * scr_cols : (i + 1) * scr_cols]
        even = scr[i, pl.ds(0, half, stride=2), :]
        odd = scr[i, pl.ds(1, half, stride=2), :]
        taps = [
            jnp.where(place == 0, 0.0, pltpu.roll(even, 1, 0)),
            jnp.where(place == 0, 0.0, pltpu.roll(odd, 1, 0)),
            even,
            odd,
            jnp.where(place == half - 1, 0.0, pltpu.roll(even, half - 1, 0)),
            jnp.where(place == half - 1, 0.0, pltpu.roll(odd, half - 1, 0)),
        ]
        for j, tap in enumerate(taps):
            at = j * cin + i * scr_cols
            taps_ref[:, at : at + scr_cols] = tap.astype(BF16)
    for copy in copies[2:]:
        copy.wait()


def activate(features, gain, weight):
    rows, cin = features.shape
    early = 2
    return pl.pallas_call(
        activate_kernel,
        out_shape=(
            jax.ShapeDtypeStruct((rows // 2, 6 * cin), BF16),
            jax.ShapeDtypeStruct((early * cin, weight.shape[2]), BF16),
        ),
        in_specs=[HBM, HBM, HBM],
        out_specs=(VMEM, VMEM),
        scratch_shapes=[
            pltpu.VMEM((rows, cin), BF16),
            pltpu.VMEM((1, cin), F32),
            pltpu.VMEM((cin // 128, rows, 128), F32),
            pltpu.SemaphoreType.DMA((2 + early,)),
        ],
        compiler_params=pltpu.CompilerParams(vmem_limit_bytes=53 * MIB),
        cost_estimate=pl.CostEstimate(flops=2 * 10**9, bytes_accessed=10**6, transcendentals=0),
        name="activate",
    )(features, gain.reshape(1, -1), weight)


def conv_kernel(
    taps_ref,
    lead_ref,
    halo_ref,
    gain_ref,
    weight_ref,
    bias_ref,
    tower_ref,
    key_ref,
    value_ref,
    normed_ref,
    packed_ref,
    rows_scr,
    weight_scr,
    sums_scr,
    pooled_scr,
    sems,
):
    taps_n, cin, depth = weight_ref.shape
    half = taps_ref.shape[0]
    early = lead_ref.shape[0] // cin
    chunk = 256
    steps = depth // chunk

    def fetch(tap):
        return pltpu.make_async_copy(
            weight_ref.at[tap + early],
            weight_scr.at[pl.ds(tap * cin, cin), :],
            sems.at[tap],
        )

    for tap in range(taps_n - early):
        fetch(tap).start()

    halo = norm_gelu(halo_ref[...].astype(F32), gain_ref[...])
    rows_scr[:half] = taps_ref[:, : taps_n * cin]
    rows_scr[half:] = taps_ref[:, cin:]
    lead = lax.broadcasted_iota(jnp.int32, (16, cin), 0)

    def put(row, at, col, value):
        old = rows_scr[at : at + 16, col : col + cin].astype(F32)
        rows_scr[at : at + 16, col : col + cin] = jnp.where(lead == row, value, old).astype(BF16)

    put(0, 0, 0, halo[0:1])
    put(0, 0, cin, halo[1:2])
    put(0, half, 0, halo[1:2])
    put(15, half - 16, 4 * cin, halo[2:3])
    put(15, 2 * half - 16, 3 * cin, halo[2:3])
    put(15, 2 * half - 16, 4 * cin, halo[3:4])

    for step in range(steps):
        cols = slice(step * chunk, (step + 1) * chunk)
        sums_scr[:, cols] = jnp.dot(
            rows_scr[:, : early * cin], lead_ref[:, cols], preferred_element_type=F32
        )
    for tap in range(taps_n - early):
        fetch(tap).wait()
    square = jnp.zeros((half, 1), F32)
    for step in range(steps):
        cols = slice(step * chunk, (step + 1) * chunk)
        both = jnp.dot(
            rows_scr[:, early * cin :], weight_scr[:, cols], preferred_element_type=F32
        )
        both = both + (sums_scr[:, cols] + bias_ref[:, cols])
        pooled = jnp.maximum(both[:half], both[half:]).astype(BF16)
        pooled_scr[:, cols] = pooled
        part = pooled.astype(F32)
        square = square + jnp.sum(part * part, axis=1, keepdims=True)
    factor = lax.rsqrt(square / (steps * chunk) + EPS)
    normed = (pooled_scr[...].astype(F32) * factor * tower_ref[...]).astype(BF16)
    normed_ref[...] = normed
    packed_ref[:half] = jnp.dot(normed, key_ref[...], preferred_element_type=F32).astype(BF16)
    values = lax.dot_general(
        normed, value_ref[...], (((1,), (1,)), ((), ())), preferred_element_type=F32
    )
    packed_ref[half : 2 * half] = values[:, :128].astype(BF16)
    rest = values[:, 128:]
    packed_ref[2 * half :] = jnp.concatenate(
        [rest[: half // 2], rest[half // 2 :]], axis=1
    ).astype(BF16)


def convolve(taps, lead, halo, conv_gain, weight, bias, tower_gain, key_weight, value_weight):
    half = taps.shape[0]
    taps_n, cin, depth = weight.shape
    rest = taps_n - lead.shape[0] // cin
    conv_gain, bias, tower_gain = (a.reshape(1, -1) for a in (conv_gain, bias, tower_gain))
    return pl.pallas_call(
        conv_kernel,
        out_shape=(
            jax.ShapeDtypeStruct((half, depth), BF16),
            jax.ShapeDtypeStruct((half * 5 // 2, 128), BF16),
        ),
        in_specs=[VMEM, VMEM, VMEM, VMEM, HBM, VMEM, VMEM, VMEM, VMEM],
        out_specs=(VMEM, VMEM),
        scratch_shapes=[
            pltpu.VMEM((2 * half, taps_n * cin), BF16),
            pltpu.VMEM((rest * cin, depth), BF16),
            pltpu.VMEM((2 * half, depth), F32),
            pltpu.VMEM((half, depth), BF16),
            pltpu.SemaphoreType.DMA((rest,)),
        ],
        compiler_params=pltpu.CompilerParams(vmem_limit_bytes=53 * MIB),
        cost_estimate=pl.CostEstimate(flops=5 * 10**9, bytes_accessed=10**7, transcendentals=0),
        name="convolve",
    )(taps, lead, halo, conv_gain, weight, bias, tower_gain, key_weight, value_weight.T)


def query_kernel(normed_ref, weight_ref, out_ref):
    rows = normed_ref.shape[0]
    chunk = 256
    for at in range(0, weight_ref.shape[1], chunk):
        result = jnp.dot(
            normed_ref[...], weight_ref[:, at : at + chunk], preferred_element_type=F32
        ).astype(BF16)
        for col in range(0, chunk, 128):
            head = (at + col) // 128
            out_ref[head * rows : (head + 1) * rows] = result[:, col : col + 128]


def project_queries(normed, weight):
    rows = normed.shape[0]
    return pl.pallas_call(
        query_kernel,
        out_shape=jax.ShapeDtypeStruct((weight.shape[1] // 128 * rows, 128), BF16),
        in_specs=[VMEM, VMEM],
        out_specs=VMEM,
        compiler_params=pltpu.CompilerParams(vmem_limit_bytes=16 * MIB),
        cost_estimate=pl.CostEstimate(flops=8 * 10**8, bytes_accessed=4 * 10**6, transcendentals=0),
        name="queries",
    )(normed, weight)


def attend_kernel(blocks, block_rows, first, last, scale, n_in, *refs):
    packed = refs[:n_in]
    q_ref = refs[n_in]
    rest = list(refs[n_in + 1 :])
    acc_ref = None if first else rest.pop(0)
    gain_ref = rest.pop(0) if last else None
    out_ref, probs, vals = rest.pop(0), rest.pop(0), rest.pop(0)
    sums = rest.pop(0) if last else out_ref
    rows = q_ref.shape[0]
    tile = probs.shape[0]
    width = block_rows * 5 // 2
    lane = lax.broadcasted_iota(jnp.int32, (block_rows // 2, 64), 1)
    ones = jnp.where(lane == 0, 1.0, 0.0).astype(BF16)
    where = []
    for ref in packed:
        for i in range(ref.shape[0] // width):
            where.append((ref, i * width))
    for j, (ref, base) in enumerate(where):
        at, mid = j * block_rows, j * block_rows + block_rows // 2
        end = at + block_rows
        vals[at:end, :128] = ref[base + block_rows : base + 2 * block_rows, :]
        tail = ref[base + 2 * block_rows : base + width, :]
        vals[at:mid, 128:] = jnp.concatenate([tail[:, :64], ones], axis=1)
        vals[mid:end, 128:] = jnp.concatenate([tail[:, 64:], ones], axis=1)

    def scores(q, j):
        ref, base = where[j]
        return (
            lax.dot_general(
                q,
                ref[base : base + block_rows, :],
                (((1,), (1,)), ((), ())),
                preferred_element_type=F32,
            )
            * scale
        )

    def weigh(q, shift):
        for j in range(len(where)):
            probs[:, j * block_rows : (j + 1) * block_rows] = jnp.exp2(
                scores(q, j) - shift
            ).astype(BF16)
        return jnp.dot(probs[...], vals[...], preferred_element_type=F32)

    column = lax.broadcasted_iota(jnp.int32, (tile, 256), 1)

    def one_tile(t, worst):
        at = pl.ds(pl.multiple_of(t * tile, tile), tile)
        q = q_ref[at, :]
        if first:
            shift = jnp.max(scores(q, 0), axis=1, keepdims=True) + SHIFT
            new = jnp.where(column == 193, shift, weigh(q, shift))
        else:
            old = acc_ref[at, :]
            new = old + weigh(q, old[:, 193:194])
        sums[at, :] = new
        return jnp.maximum(worst, jnp.where(new[:, 192:193] <= BIG, 0.0, 1.0))

    worst = lax.fori_loop(0, rows // tile, one_tile, jnp.zeros((tile, 1), F32))

    def redo(t, _):
        at = pl.ds(pl.multiple_of(t * tile, tile), tile)
        q = q_ref[at, :]
        top = jnp.max(scores(q, 0), axis=1, keepdims=True)
        for j in range(1, len(where)):
            top = jnp.maximum(top, jnp.max(scores(q, j), axis=1, keepdims=True))
        top = top + SHIFT
        if first:
            again = weigh(q, top)
        else:
            shift = acc_ref[at, 193:194]
            top = jnp.maximum(top, shift)
            again = weigh(q, top) + acc_ref[at, :] * jnp.exp2(shift - top)
        sums[at, :] = jnp.where(column == 193, top, again)
        return 0

    @pl.when(jnp.max(worst) > 0.0)
    def _():
        lax.fori_loop(0, rows // tile, redo, 0)

    if last:
        heads = rows // block_rows
        step = 64
        sem = rest.pop(0)
        stage = rest.pop(0)
        copies = []
        for r in range(0, block_rows, step):
            square = jnp.zeros((step, 1), F32)
            inverse = []
            for h in range(heads):
                at = slice(h * block_rows + r, h * block_rows + r + step)
                part = sums[at, :192]
                inverse.append(1.0 / sums[at, 192:193])
                size = jnp.sum(part * part, axis=1, keepdims=True)
                square = square + size * inverse[h] * inverse[h]
            factor = lax.rsqrt(square / (heads * 192) + EPS)
            for h in range(0, heads, 2):
                pair = [
                    sums[i * block_rows + r : i * block_rows + r + step, :192]
                    * (inverse[i] * factor)
                    for i in (h, h + 1)
                ]
                cols = slice(h * 192, (h + 2) * 192)
                stage[r : r + step, cols] = jnp.concatenate(pair, axis=1) * gain_ref[:, cols]
            copies.append(
                pltpu.make_async_copy(
                    stage.at[pl.ds(r, step)], out_ref.at[pl.ds(r, step)], sem.at[r // step]
                )
            )
            copies[-1].start()
        for copy in copies:
            copy.wait()


def attend(packed, queries, acc, block_rows, scale, out_gain=None):
    first, last = acc is None, out_gain is not None
    width = block_rows * 5 // 2
    blocks = sum(p.shape[0] for p in packed) // width
    rows = queries.shape[0]
    tile = 1024
    args = list(packed) + [queries]
    if not first:
        args.append(acc)
    if last:
        args.append(out_gain.reshape(1, -1))
    out = (block_rows, rows // block_rows * 192) if last else (rows, 256)
    keys = blocks * block_rows
    scratch = [pltpu.VMEM((tile, keys), BF16), pltpu.VMEM((keys, 256), BF16)]
    if last:
        scratch += [
            pltpu.VMEM((rows, 256), F32),
            pltpu.SemaphoreType.DMA((block_rows // 64,)),
            pltpu.VMEM(out, F32),
        ]
    return pl.pallas_call(
        functools.partial(attend_kernel, blocks, block_rows, first, last, scale, len(packed)),
        out_shape=jax.ShapeDtypeStruct(out, F32),
        in_specs=[VMEM] * len(args),
        out_specs=HBM if last else VMEM,
        scratch_shapes=scratch,
        compiler_params=pltpu.CompilerParams(vmem_limit_bytes=36 * MIB),
        cost_estimate=pl.CostEstimate(
            flops=rows * keys * 640, bytes_accessed=10**6, transcendentals=0
        ),
        name="attend",
    )(*args)


def ring_moves():
    every = [(y, z, c) for y in range(2) for z in range(8) for c in range(2)]
    at = lambda y, z, c: y * 16 + (z % 8) * 2 + c

    def along_z(step):
        return [(at(y, z, c), at(y, z + (step if c == 0 else -step), c)) for y, z, c in every]

    across = [(at(y, z, c), at(1 - y, z, c)) for y, z, c in every]
    other = [(at(y, z, c), at(y, z, 1 - c)) for y, z, c in every]
    return along_z, across, other


def shards(
    features,
    conv_gain,
    conv_weight,
    conv_bias,
    tower_gain,
    query_weight,
    key_weight,
    value_weight,
    out_gain,
):
    count = lax.axis_size("seq")
    before = lax.ppermute(features[-2:], "seq", [(i, i + 1) for i in range(count - 1)])
    after = lax.ppermute(features[:2], "seq", [(i + 1, i) for i in range(count - 1)])
    taps, lead = activate(features, conv_gain, conv_weight)
    halo = jnp.concatenate([before, after], axis=0)
    normed, own = convolve(
        taps, lead, halo, conv_gain, conv_weight, conv_bias, tower_gain, key_weight, value_weight
    )
    along_z, across, other = ring_moves()
    z = lambda block, step: lax.ppermute(block, "seq", along_z(step))
    y = lambda block: lax.ppermute(block, "seq", across)
    c = lambda block: lax.ppermute(block, "seq", other)
    hold = lax.optimization_barrier
    block_rows = normed.shape[0]
    scale = math.log2(math.e) / math.sqrt(key_weight.shape[1])
    own_c = c(own)
    y0 = y(own)
    chip = jnp.concatenate([own, own_c], axis=0)
    z1 = z(chip, 1)
    z2 = z(chip, 2)
    queries = project_queries(normed, query_weight)
    part = functools.partial(attend, queries=queries, block_rows=block_rows, scale=scale)
    y0, queries = hold((y0, queries))
    y0_c = c(y0)
    part = functools.partial(attend, queries=queries, block_rows=block_rows, scale=scale)
    yz1 = z(jnp.concatenate([y0, y0_c], axis=0), 1)
    acc = part([own, own_c, y0, y0_c], acc=None)
    z1, z2, acc = hold((z1, z2, acc))
    z3 = z(z2, 1)
    y2 = y(z2)
    z4 = z(z2[: own.shape[0]], 2)
    acc = part([z1, c(z1), z2, c(z2)], acc=acc)
    z3, z4, yz1, y2, acc = hold((z3, z4, yz1, y2, acc))
    y3, y4 = y(z3), y(z4)
    acc = part([z3, c(z3), z4, c(z4), yz1, c(yz1), y2, c(y2)], acc=acc)
    y3, y4, acc = hold((y3, y4, acc))
    return part([y3, c(y3), y4, c(y4)], acc=acc, out_gain=out_gain)


def solution(mesh):
    placed = (P(("dp", "seq"), None), P(), P(), P(), P(), P(), P(), P(), P())
    return jax.shard_map(
        shards, mesh=mesh, in_specs=placed, out_specs=P(("dp", "seq"), None), check_vma=False
    )
```

```python
import functools
import math

import jax
import jax.numpy as jnp
from jax import lax
from jax.experimental import pallas as pl
from jax.experimental.pallas import tpu as pltpu
from jax.sharding import PartitionSpec as P

F32 = jnp.float32
BF16 = jnp.bfloat16
EPS = 1e-06
MIB = 2**20
CONV_LIMIT = 52
SHIFT = 32.0
BIG = 2.0**100
VMEM = pl.BlockSpec(memory_space=pltpu.VMEM)
HBM = pl.BlockSpec(memory_space=pltpu.HBM)


def norm_gelu(rows, gain):
    mean_sq = jnp.mean(rows * rows, axis=-1, keepdims=True)
    normed = rows * lax.rsqrt(mean_sq + EPS) * gain
    return 0.5 * normed * (1.0 + lax.erf(normed * math.sqrt(0.5)))


PHASES = ((0, 1), (1, 3), (3, 5))


def activate_kernel(feat_ref, gain_ref, taps_ref, scr):
    rows, cin = feat_ref.shape
    half = rows // 2
    active = norm_gelu(feat_ref[...].astype(F32), gain_ref[...])
    place = lax.broadcasted_iota(jnp.int32, (half, 128), 0)
    for i in range(cin // 128):
        scr[i] = active[:, i * 128 : (i + 1) * 128]
        even = scr[i, pl.ds(0, half, stride=2), :]
        odd = scr[i, pl.ds(1, half, stride=2), :]
        taps = [
            jnp.where(place == 0, 0.0, pltpu.roll(even, 1, 0)),
            jnp.where(place == 0, 0.0, pltpu.roll(odd, 1, 0)),
            even,
            odd,
            jnp.where(place == half - 1, 0.0, pltpu.roll(even, half - 1, 0)),
            jnp.where(place == half - 1, 0.0, pltpu.roll(odd, half - 1, 0)),
        ]
        for j, tap in enumerate(taps):
            at = j * cin + i * 128
            taps_ref[:, at : at + 128] = tap.astype(BF16)


def activate(features, gain):
    rows, cin = features.shape
    return pl.pallas_call(
        activate_kernel,
        out_shape=jax.ShapeDtypeStruct((rows // 2, 6 * cin), BF16),
        in_specs=[VMEM, VMEM],
        out_specs=VMEM,
        scratch_shapes=[pltpu.VMEM((cin // 128, rows, 128), F32)],
        compiler_params=pltpu.CompilerParams(vmem_limit_bytes=8 * MIB),
        cost_estimate=pl.CostEstimate(flops=10**9, bytes_accessed=10**6, transcendentals=0),
        name="activate",
    )(features, gain)


def conv_kernel(
    taps_ref,
    halo_ref,
    gain_ref,
    weight_ref,
    bias_ref,
    tower_ref,
    normed_ref,
    rows_scr,
    weight_scr,
    sums_scr,
    pooled_scr,
    sems,
):
    taps_n, cin, depth = weight_ref.shape
    half = taps_ref.shape[0]
    chunk = 256
    steps = depth // chunk

    def fetch(tap):
        return pltpu.make_async_copy(
            weight_ref.at[tap], weight_scr.at[pl.ds(tap * cin, cin), :], sems.at[tap]
        )

    for tap in range(taps_n):
        fetch(tap).start()

    rows_scr[:half] = taps_ref[:, : taps_n * cin]
    rows_scr[half:] = taps_ref[:, cin:]
    halo = norm_gelu(halo_ref[...].astype(F32), gain_ref[...])
    lead = lax.broadcasted_iota(jnp.int32, (16, cin), 0)

    def put(row, at, col, value):
        old = rows_scr[at : at + 16, col : col + cin].astype(F32)
        rows_scr[at : at + 16, col : col + cin] = jnp.where(lead == row, value, old).astype(BF16)

    put(0, 0, 0, halo[0:1])
    put(0, 0, cin, halo[1:2])
    put(0, half, 0, halo[1:2])
    put(15, half - 16, 4 * cin, halo[2:3])
    put(15, 2 * half - 16, 3 * cin, halo[2:3])
    put(15, 2 * half - 16, 4 * cin, halo[3:4])

    square = jnp.zeros((half, 1), F32)
    for begin, end in PHASES:
        for tap in range(begin, end):
            fetch(tap).wait()
        deep = slice(begin * cin, end * cin)
        for step in range(steps):
            cols = slice(step * chunk, (step + 1) * chunk)
            both = jnp.dot(rows_scr[:, deep], weight_scr[deep, cols], preferred_element_type=F32)
            both = both + (bias_ref[:, cols] if begin == 0 else sums_scr[:, cols])
            if end < taps_n:
                sums_scr[:, cols] = both
            else:
                pooled = jnp.maximum(both[:half], both[half:]).astype(BF16)
                pooled_scr[:, cols] = pooled
                part = pooled.astype(F32)
                square = square + jnp.sum(part * part, axis=1, keepdims=True)
    factor = lax.rsqrt(square / depth + EPS)
    normed_ref[...] = (pooled_scr[...].astype(F32) * factor * tower_ref[...]).astype(BF16)


def convolve(taps, halo, conv_gain, weight, bias, tower_gain):
    half = taps.shape[0]
    taps_n, cin, depth = weight.shape
    return pl.pallas_call(
        conv_kernel,
        out_shape=jax.ShapeDtypeStruct((half, depth), BF16),
        in_specs=[VMEM, VMEM, VMEM, HBM, VMEM, VMEM],
        out_specs=VMEM,
        scratch_shapes=[
            pltpu.VMEM((2 * half, taps_n * cin), BF16),
            pltpu.VMEM((taps_n * cin, depth), BF16),
            pltpu.VMEM((2 * half, depth), F32),
            pltpu.VMEM((half, depth), BF16),
            pltpu.SemaphoreType.DMA((taps_n,)),
        ],
        compiler_params=pltpu.CompilerParams(vmem_limit_bytes=CONV_LIMIT * MIB),
        cost_estimate=pl.CostEstimate(flops=5 * 10**9, bytes_accessed=10**7, transcendentals=0),
        name="convolve",
    )(taps, halo, conv_gain, weight, bias, tower_gain)


def pack_kernel(normed_ref, key_ref, value_ref, packed_ref):
    half = normed_ref.shape[0]
    normed = normed_ref[...]
    packed_ref[:half] = jnp.dot(normed, key_ref[...], preferred_element_type=F32).astype(BF16)
    values = lax.dot_general(
        normed, value_ref[...], (((1,), (1,)), ((), ())), preferred_element_type=F32
    )
    packed_ref[half : 2 * half] = values[:, :128].astype(BF16)
    rest = values[:, 128:]
    packed_ref[2 * half :] = jnp.concatenate(
        [rest[: half // 2], rest[half // 2 :]], axis=1
    ).astype(BF16)


def pack_keys_values(normed, key_weight, value_weight):
    return pl.pallas_call(
        pack_kernel,
        out_shape=jax.ShapeDtypeStruct((normed.shape[0] * 5 // 2, 128), BF16),
        in_specs=[VMEM] * 3,
        out_specs=VMEM,
        compiler_params=pltpu.CompilerParams(vmem_limit_bytes=8 * MIB),
        cost_estimate=pl.CostEstimate(flops=2 * 10**8, bytes_accessed=10**6, transcendentals=0),
        name="pack",
    )(normed, key_weight, value_weight.T)


def query_kernel(normed_ref, weight_ref, out_ref):
    rows = normed_ref.shape[0]
    chunk = 256
    for at in range(0, weight_ref.shape[1], chunk):
        result = jnp.dot(
            normed_ref[...], weight_ref[:, at : at + chunk], preferred_element_type=F32
        ).astype(BF16)
        for col in range(0, chunk, 128):
            head = (at + col) // 128
            out_ref[head * rows : (head + 1) * rows] = result[:, col : col + 128]


def project_queries(normed, weight):
    rows = normed.shape[0]
    return pl.pallas_call(
        query_kernel,
        out_shape=jax.ShapeDtypeStruct((weight.shape[1] // 128 * rows, 128), BF16),
        in_specs=[VMEM, VMEM],
        out_specs=VMEM,
        compiler_params=pltpu.CompilerParams(vmem_limit_bytes=16 * MIB),
        cost_estimate=pl.CostEstimate(flops=8 * 10**8, bytes_accessed=4 * 10**6, transcendentals=0),
        name="queries",
    )(normed, weight)


def attend_kernel(blocks, block_rows, first, last, scale, n_in, *refs):
    packed = refs[:n_in]
    q_ref = refs[n_in]
    rest = list(refs[n_in + 1 :])
    acc_ref = None if first else rest.pop(0)
    gain_ref = rest.pop(0) if last else None
    out_ref, probs, keys, vals = rest.pop(0), rest.pop(0), rest.pop(0), rest.pop(0)
    sums = rest.pop(0) if last else out_ref
    rows = q_ref.shape[0]
    tile = probs.shape[0]
    width = block_rows * 5 // 2
    lane = lax.broadcasted_iota(jnp.int32, (block_rows // 2, 64), 1)
    ones = jnp.where(lane == 0, 1.0, 0.0).astype(BF16)
    at = 0
    for ref in packed:
        for base in range(0, ref.shape[0], width):
            mid, end = at + block_rows // 2, at + block_rows
            keys[at:end] = ref[base : base + block_rows, :]
            vals[at:end, :128] = ref[base + block_rows : base + 2 * block_rows, :]
            tail = ref[base + 2 * block_rows : base + width, :]
            vals[at:mid, 128:] = jnp.concatenate([tail[:, :64], ones], axis=1)
            vals[mid:end, 128:] = jnp.concatenate([tail[:, 64:], ones], axis=1)
            at = end

    def scores(q, at):
        part = lax.dot_general(
            q, keys[at, :], (((1,), (1,)), ((), ())), preferred_element_type=F32
        )
        return part * scale

    def weigh(q, shift):
        for j in range(blocks):
            at = slice(j * block_rows, (j + 1) * block_rows)
            probs[:, at] = jnp.exp2(scores(q, at) - shift).astype(BF16)
        return jnp.dot(probs[...], vals[...], preferred_element_type=F32)

    column = lax.broadcasted_iota(jnp.int32, (tile, 256), 1)

    def one_tile(t, worst):
        at = slice(t * tile, (t + 1) * tile)
        q = q_ref[at, :]
        if first:
            shift = jnp.max(scores(q, slice(0, block_rows)), axis=1, keepdims=True) + SHIFT
            new = jnp.where(column == 193, shift, weigh(q, shift))
        else:
            old = acc_ref[at, :]
            new = old + weigh(q, old[:, 193:194])
        sums[at, :] = new
        return jnp.maximum(worst, jnp.where(new[:, 192:193] <= BIG, 0.0, 1.0))

    worst = jnp.zeros((tile, 1), F32)
    for t in range(rows // tile):
        worst = one_tile(t, worst)

    def redo(t, _):
        at = pl.ds(pl.multiple_of(t * 128, 128), 128)
        q = q_ref[at, :]

        def block(j):
            return pl.ds(pl.multiple_of(j * block_rows, block_rows), block_rows)

        def higher(j, top):
            return jnp.maximum(top, jnp.max(scores(q, block(j)), axis=1, keepdims=True) + SHIFT)

        old = jnp.full((128, 1), -jnp.inf, F32) if first else acc_ref[at, 193:194]
        top = lax.fori_loop(0, blocks, higher, old)

        def add(j, total):
            part = jnp.exp2(scores(q, block(j)) - top).astype(BF16)
            return total + jnp.dot(part, vals[block(j), :], preferred_element_type=F32)

        start = jnp.zeros((128, 256), F32) if first else acc_ref[at, :] * jnp.exp2(old - top)
        total = lax.fori_loop(0, blocks, add, start)
        sums[at, :] = jnp.where(column[:128] == 193, top, total)
        return 0

    @pl.when(jnp.max(worst) > 0.0)
    def _():
        lax.fori_loop(0, rows // 128, redo, 0)

    if last:
        heads = rows // block_rows
        step = 64
        sem = rest.pop(0)
        stage = rest.pop(0)
        square = jnp.zeros((block_rows, 1), F32)
        inverse = []
        for h in range(heads):
            at = slice(h * block_rows, (h + 1) * block_rows)
            part = sums[at, :192]
            inverse.append(1.0 / sums[at, 192:193])
            size = jnp.sum(part * part, axis=1, keepdims=True)
            square = square + size * inverse[h] * inverse[h]
        factor = lax.rsqrt(square / (heads * 192) + EPS)
        inverse = [i * factor for i in inverse]
        copies = []
        for r in range(0, block_rows, step):
            for h in range(0, heads, 2):
                pair = [
                    sums[i * block_rows + r : i * block_rows + r + step, :192]
                    * inverse[i][r : r + step]
                    for i in (h, h + 1)
                ]
                cols = slice(h * 192, (h + 2) * 192)
                stage[r : r + step, cols] = jnp.concatenate(pair, axis=1) * gain_ref[:, cols]
            copies.append(
                pltpu.make_async_copy(
                    stage.at[pl.ds(r, step)], out_ref.at[pl.ds(r, step)], sem.at[r // step]
                )
            )
            copies[-1].start()
        for copy in copies:
            copy.wait()


def attend(packed, queries, acc, *, block_rows, scale, out_gain=None, cost=640):
    first, last = acc is None, out_gain is not None
    width = block_rows * 5 // 2
    blocks = sum(p.shape[0] for p in packed) // width
    rows = queries.shape[0]
    tile = 1024
    args = list(packed) + [queries]
    if not first:
        args.append(acc)
    if last:
        args.append(out_gain.reshape(1, -1))
    out = (block_rows, rows // block_rows * 192) if last else (rows, 256)
    keys = blocks * block_rows
    scratch = [
        pltpu.VMEM((tile, keys), BF16),
        pltpu.VMEM((keys, 128), BF16),
        pltpu.VMEM((keys, 256), BF16),
    ]
    if last:
        scratch += [
            pltpu.VMEM((rows, 256), F32),
            pltpu.SemaphoreType.DMA((block_rows // 64,)),
            pltpu.VMEM(out, F32),
        ]
    return pl.pallas_call(
        functools.partial(attend_kernel, blocks, block_rows, first, last, scale, len(packed)),
        out_shape=jax.ShapeDtypeStruct(out, F32),
        in_specs=[VMEM] * len(args),
        out_specs=HBM if last else VMEM,
        scratch_shapes=scratch,
        compiler_params=pltpu.CompilerParams(vmem_limit_bytes=36 * MIB),
        cost_estimate=pl.CostEstimate(
            flops=rows * keys * cost, bytes_accessed=10**6, transcendentals=0
        ),
        name="attend",
    )(*args)


def ring_moves():
    every = [(y, z, c) for y in range(2) for z in range(8) for c in range(2)]
    at = lambda y, z, c: y * 16 + (z % 8) * 2 + c

    def along_z(step):
        return [(at(y, z, c), at(y, z + (step if c == 0 else -step), c)) for y, z, c in every]

    across = [(at(y, z, c), at(1 - y, z, c)) for y, z, c in every]
    other = [(at(y, z, c), at(y, z, 1 - c)) for y, z, c in every]
    return along_z, across, other


def shards(
    features,
    conv_gain,
    conv_weight,
    conv_bias,
    tower_gain,
    query_weight,
    key_weight,
    value_weight,
    out_gain,
):
    count = lax.axis_size("seq")
    before = lax.ppermute(features[-2:], "seq", [(i, i + 1) for i in range(count - 1)])
    after = lax.ppermute(features[:2], "seq", [(i + 1, i) for i in range(count - 1)])
    gain = conv_gain.reshape(1, -1)
    taps = activate(features, gain)
    halo = jnp.concatenate([before, after], axis=0)
    normed = convolve(
        taps, halo, gain, conv_weight, conv_bias.reshape(1, -1), tower_gain.reshape(1, -1)
    )
    own = pack_keys_values(normed, key_weight, value_weight)
    along_z, across, other = ring_moves()
    z = lambda block, step: lax.ppermute(block, "seq", along_z(step))
    y = lambda block: lax.ppermute(block, "seq", across)
    c = lambda block: lax.ppermute(block, "seq", other)
    hold = lax.optimization_barrier
    block_rows = normed.shape[0]
    scale = math.log2(math.e) / math.sqrt(key_weight.shape[1])
    own_c = c(own)
    cat = lambda *blocks: jnp.concatenate(blocks, axis=0)
    chip = cat(own, own_c)
    z2 = z(chip, 2)
    z1 = z(chip, 1)
    y0 = y(own)
    queries = project_queries(normed, query_weight)
    part = functools.partial(attend, block_rows=block_rows, scale=scale)
    acc = part([own, own_c], queries, None, cost=640)
    y0, acc = hold((y0, acc))
    y0_c = c(y0)
    yz1 = z(cat(y0, y0_c), 1)
    acc = part([y0, y0_c], queries, acc, cost=640)
    z2, acc = hold((z2, acc))
    half_z2 = z2[: own.shape[0]]
    z4 = z(half_z2, 2)
    z3 = z(z2, 1)
    y2 = y(z2)
    z2_c = c(z2)
    z1, z2_c, acc = hold((z1, z2_c, acc))
    z1_c = c(z1)
    acc = part([z2, z2_c, z1], queries, acc, cost=640)
    z1_c, z3, acc = hold((z1_c, z3, acc))
    y3 = y(z3)
    acc = part([z1_c], queries, acc, cost=6400)
    z4, y2, acc = hold((z4, y2, acc))
    y4 = y(z4)
    near = cat(z3, z4, y2, yz1)
    near_c = c(near)
    acc = part([near], queries, acc, cost=6400)
    acc = part([near_c], queries, acc, cost=6400)
    y3, y4, acc = hold((y3, y4, acc))
    last = cat(y3, y4)
    last_c = c(last)
    acc = part([last], queries, acc, cost=6400)
    return part([last_c], queries, acc, out_gain=out_gain)


def solution(mesh):
    placed = (P(("dp", "seq"), None), P(), P(), P(), P(), P(), P(), P(), P())
    return jax.shard_map(
        shards, mesh=mesh, in_specs=placed, out_specs=P(("dp", "seq"), None), check_vma=False
    )
```

```python
import functools
import math

import jax
import jax.numpy as jnp
from jax import lax
from jax.experimental import pallas as pl
from jax.experimental.pallas import tpu as pltpu
from jax.sharding import PartitionSpec as P

F32 = jnp.float32
BF16 = jnp.bfloat16
EPS = 1e-06
MIB = 2**20
CONV_LIMIT = 50
SHIFT = 32.0
BIG = 2.0**100
VMEM = pl.BlockSpec(memory_space=pltpu.VMEM)
HBM = pl.BlockSpec(memory_space=pltpu.HBM)


def norm_gelu(rows, gain):
    mean_sq = jnp.mean(rows * rows, axis=-1, keepdims=True)
    normed = rows * lax.rsqrt(mean_sq + EPS) * gain
    return 0.5 * normed * (1.0 + lax.erf(normed * math.sqrt(0.5)))


PHASES = ((0, 1), (1, 3), (3, 5))


def activate_kernel(feat_ref, gain_ref, taps_ref, scr):
    rows, cin = feat_ref.shape
    half = rows // 2
    active = norm_gelu(feat_ref[...].astype(F32), gain_ref[...])
    place = lax.broadcasted_iota(jnp.int32, (half, 128), 0)
    for i in range(cin // 128):
        scr[i] = active[:, i * 128 : (i + 1) * 128]
        even = scr[i, pl.ds(0, half, stride=2), :]
        odd = scr[i, pl.ds(1, half, stride=2), :]
        taps = [
            jnp.where(place == 0, 0.0, pltpu.roll(even, 1, 0)),
            jnp.where(place == 0, 0.0, pltpu.roll(odd, 1, 0)),
            even,
            odd,
            jnp.where(place == half - 1, 0.0, pltpu.roll(even, half - 1, 0)),
            jnp.where(place == half - 1, 0.0, pltpu.roll(odd, half - 1, 0)),
        ]
        for j, tap in enumerate(taps):
            at = j * cin + i * 128
            taps_ref[:, at : at + 128] = tap.astype(BF16)


def activate(features, gain):
    rows, cin = features.shape
    return pl.pallas_call(
        activate_kernel,
        out_shape=jax.ShapeDtypeStruct((rows // 2, 6 * cin), BF16),
        in_specs=[VMEM, VMEM],
        out_specs=VMEM,
        scratch_shapes=[pltpu.VMEM((cin // 128, rows, 128), F32)],
        compiler_params=pltpu.CompilerParams(vmem_limit_bytes=8 * MIB),
        cost_estimate=pl.CostEstimate(flops=10**9, bytes_accessed=10**6, transcendentals=0),
        name="activate",
    )(features, gain)


def conv_kernel(
    taps_ref,
    halo_ref,
    gain_ref,
    weight_ref,
    bias_ref,
    tower_ref,
    normed_ref,
    rows_scr,
    weight_scr,
    sums_scr,
    pooled_scr,
    sems,
):
    taps_n, cin, depth = weight_ref.shape
    half = taps_ref.shape[0]
    chunk = 256
    steps = depth // chunk

    def fetch(tap):
        return pltpu.make_async_copy(
            weight_ref.at[tap], weight_scr.at[pl.ds(tap * cin, cin), :], sems.at[tap]
        )

    for tap in range(taps_n):
        fetch(tap).start()

    rows_scr[:half] = taps_ref[:, : taps_n * cin]
    rows_scr[half:] = taps_ref[:, cin:]
    halo = norm_gelu(halo_ref[...].astype(F32), gain_ref[...])
    lead = lax.broadcasted_iota(jnp.int32, (16, cin), 0)

    def put(row, at, col, value):
        old = rows_scr[at : at + 16, col : col + cin].astype(F32)
        rows_scr[at : at + 16, col : col + cin] = jnp.where(lead == row, value, old).astype(BF16)

    put(0, 0, 0, halo[0:1])
    put(0, 0, cin, halo[1:2])
    put(0, half, 0, halo[1:2])
    put(15, half - 16, 4 * cin, halo[2:3])
    put(15, 2 * half - 16, 3 * cin, halo[2:3])
    put(15, 2 * half - 16, 4 * cin, halo[3:4])

    square = jnp.zeros((half, 1), F32)
    for begin, end in PHASES:
        for tap in range(begin, end):
            fetch(tap).wait()
        deep = slice(begin * cin, end * cin)
        for step in range(steps):
            cols = slice(step * chunk, (step + 1) * chunk)
            both = jnp.dot(rows_scr[:, deep], weight_scr[deep, cols], preferred_element_type=F32)
            both = both + (bias_ref[:, cols] if begin == 0 else sums_scr[:, cols])
            if end < taps_n:
                sums_scr[:, cols] = both
            else:
                pooled = jnp.maximum(both[:half], both[half:]).astype(BF16)
                pooled_scr[:, cols] = pooled
                part = pooled.astype(F32)
                square = square + jnp.sum(part * part, axis=1, keepdims=True)
    factor = lax.rsqrt(square / depth + EPS)
    normed_ref[...] = (pooled_scr[...].astype(F32) * factor * tower_ref[...]).astype(BF16)


def convolve(taps, halo, conv_gain, weight, bias, tower_gain):
    half = taps.shape[0]
    taps_n, cin, depth = weight.shape
    return pl.pallas_call(
        conv_kernel,
        out_shape=jax.ShapeDtypeStruct((half, depth), BF16),
        in_specs=[VMEM, VMEM, VMEM, HBM, VMEM, VMEM],
        out_specs=VMEM,
        scratch_shapes=[
            pltpu.VMEM((2 * half, taps_n * cin), BF16),
            pltpu.VMEM((taps_n * cin, depth), BF16),
            pltpu.VMEM((2 * half, depth), F32),
            pltpu.VMEM((half, depth), BF16),
            pltpu.SemaphoreType.DMA((taps_n,)),
        ],
        compiler_params=pltpu.CompilerParams(vmem_limit_bytes=CONV_LIMIT * MIB),
        cost_estimate=pl.CostEstimate(flops=5 * 10**9, bytes_accessed=10**7, transcendentals=0),
        name="convolve",
    )(taps, halo, conv_gain, weight, bias, tower_gain)


def pack_kernel(normed_ref, key_ref, value_ref, packed_ref):
    half = normed_ref.shape[0]
    normed = normed_ref[...]
    packed_ref[:half] = jnp.dot(normed, key_ref[...], preferred_element_type=F32).astype(BF16)
    values = lax.dot_general(
        normed, value_ref[...], (((1,), (1,)), ((), ())), preferred_element_type=F32
    )
    packed_ref[half : 2 * half] = values[:, :128].astype(BF16)
    rest = values[:, 128:]
    packed_ref[2 * half :] = jnp.concatenate(
        [rest[: half // 2], rest[half // 2 :]], axis=1
    ).astype(BF16)


def pack_keys_values(normed, key_weight, value_weight):
    return pl.pallas_call(
        pack_kernel,
        out_shape=jax.ShapeDtypeStruct((normed.shape[0] * 5 // 2, 128), BF16),
        in_specs=[VMEM] * 3,
        out_specs=VMEM,
        compiler_params=pltpu.CompilerParams(vmem_limit_bytes=8 * MIB),
        cost_estimate=pl.CostEstimate(flops=2 * 10**8, bytes_accessed=10**6, transcendentals=0),
        name="pack",
    )(normed, key_weight, value_weight.T)


def query_kernel(normed_ref, weight_ref, out_ref):
    rows = normed_ref.shape[0]
    chunk = 256
    for at in range(0, weight_ref.shape[1], chunk):
        result = jnp.dot(
            normed_ref[...], weight_ref[:, at : at + chunk], preferred_element_type=F32
        ).astype(BF16)
        for col in range(0, chunk, 128):
            head = (at + col) // 128
            out_ref[head * rows : (head + 1) * rows] = result[:, col : col + 128]


def project_queries(normed, weight):
    rows = normed.shape[0]
    return pl.pallas_call(
        query_kernel,
        out_shape=jax.ShapeDtypeStruct((weight.shape[1] // 128 * rows, 128), BF16),
        in_specs=[VMEM, VMEM],
        out_specs=VMEM,
        compiler_params=pltpu.CompilerParams(vmem_limit_bytes=16 * MIB),
        cost_estimate=pl.CostEstimate(flops=8 * 10**8, bytes_accessed=4 * 10**6, transcendentals=0),
        name="queries",
    )(normed, weight)


def attend_kernel(blocks, block_rows, first, last, scale, n_in, *refs):
    packed = refs[:n_in]
    q_ref = refs[n_in]
    rest = list(refs[n_in + 1 :])
    acc_ref = None if first else rest.pop(0)
    gain_ref = rest.pop(0) if last else None
    out_ref, probs, keys, vals = rest.pop(0), rest.pop(0), rest.pop(0), rest.pop(0)
    sums = rest.pop(0) if last else out_ref
    rows = q_ref.shape[0]
    tile = probs.shape[0]
    width = block_rows * 5 // 2
    ones = jnp.ones((block_rows // 2, 64), BF16)
    at = 0
    for ref in packed:
        for base in range(0, ref.shape[0], width):
            mid, end = at + block_rows // 2, at + block_rows
            keys[at:end] = ref[base : base + block_rows, :]
            vals[at:end, :128] = ref[base + block_rows : base + 2 * block_rows, :]
            tail = ref[base + 2 * block_rows : base + width, :]
            vals[at:mid, 128:] = jnp.concatenate([tail[:, :64], ones], axis=1)
            vals[mid:end, 128:] = jnp.concatenate([tail[:, 64:], ones], axis=1)
            at = end

    def scores(q, at):
        part = lax.dot_general(
            q, keys[at, :], (((1,), (1,)), ((), ())), preferred_element_type=F32
        )
        return part * scale

    def weigh(q, shift):
        for j in range(blocks):
            at = slice(j * block_rows, (j + 1) * block_rows)
            probs[:, at] = jnp.exp2(scores(q, at) - shift).astype(BF16)
        return jnp.dot(probs[...], vals[...], preferred_element_type=F32)

    def one_tile(t, worst):
        at = slice(t * tile, (t + 1) * tile)
        q = q_ref[at, :]
        if first:
            top = jnp.max(scores(q, slice(0, block_rows)), axis=1, keepdims=True)
            shift = jnp.broadcast_to(top + SHIFT, (tile, 128))
        else:
            shift = acc_ref[at, 256:]
        new = weigh(q, jnp.concatenate([shift] * (block_rows // 128), axis=1))
        if not first:
            new = new + acc_ref[at, :256]
        sums[at, :256] = new
        sums[at, 256:] = shift
        return jnp.maximum(worst, jnp.where(new[:, 128:] <= BIG, 0.0, 1.0))

    worst = jnp.zeros((tile, 128), F32)
    for t in range(rows // tile):
        worst = one_tile(t, worst)

    def redo(t, _):
        at = pl.ds(pl.multiple_of(t * 128, 128), 128)
        q = q_ref[at, :]

        def block(j):
            return pl.ds(pl.multiple_of(j * block_rows, block_rows), block_rows)

        def higher(j, top):
            return jnp.maximum(top, jnp.max(scores(q, block(j)), axis=1, keepdims=True) + SHIFT)

        old = jnp.full((128, 1), -jnp.inf, F32) if first else acc_ref[at, 256:257]
        top = lax.fori_loop(0, blocks, higher, old)

        def add(j, total):
            part = jnp.exp2(scores(q, block(j)) - top).astype(BF16)
            return total + jnp.dot(part, vals[block(j), :], preferred_element_type=F32)

        start = jnp.zeros((128, 256), F32) if first else acc_ref[at, :256] * jnp.exp2(old - top)
        total = lax.fori_loop(0, blocks, add, start)
        sums[at, :256] = total
        sums[at, 256:] = jnp.broadcast_to(top, (128, 128))
        return 0

    @pl.when(jnp.max(worst) > 0.0)
    def _():
        lax.fori_loop(0, rows // 128, redo, 0)

    if last:
        heads = rows // block_rows
        step = 128
        sem = rest.pop(0)
        stage = rest.pop(0)
        square = jnp.zeros((block_rows, 1), F32)
        inverse = []
        for h in range(heads):
            at = slice(h * block_rows, (h + 1) * block_rows)
            part = sums[at, :192]
            inverse.append(1.0 / sums[at, 192:193])
            size = jnp.sum(part * part, axis=1, keepdims=True)
            square = square + size * inverse[h] * inverse[h]
        factor = lax.rsqrt(square / (heads * 192) + EPS)
        inverse = [i * factor for i in inverse]
        copies = []
        for r in range(0, block_rows, step):
            for h in range(0, heads, 2):
                pair = [
                    sums[i * block_rows + r : i * block_rows + r + step, :192]
                    * inverse[i][r : r + step]
                    for i in (h, h + 1)
                ]
                cols = slice(h * 192, (h + 2) * 192)
                stage[r : r + step, cols] = jnp.concatenate(pair, axis=1) * gain_ref[:, cols]
            copies.append(
                pltpu.make_async_copy(
                    stage.at[pl.ds(r, step)], out_ref.at[pl.ds(r, step)], sem.at[r // step]
                )
            )
            copies[-1].start()
        for copy in copies:
            copy.wait()


def attend(packed, queries, acc, *, block_rows, scale, out_gain=None, cost=640):
    first, last = acc is None, out_gain is not None
    width = block_rows * 5 // 2
    blocks = sum(p.shape[0] for p in packed) // width
    rows = queries.shape[0]
    tile = 1024
    args = list(packed) + [queries]
    if not first:
        args.append(acc)
    if last:
        args.append(out_gain.reshape(1, -1))
    out = (block_rows, rows // block_rows * 192) if last else (rows, 384)
    keys = blocks * block_rows
    scratch = [
        pltpu.VMEM((tile, keys), BF16),
        pltpu.VMEM((keys, 128), BF16),
        pltpu.VMEM((keys, 256), BF16),
    ]
    if last:
        scratch += [
            pltpu.VMEM((rows, 384), F32),
            pltpu.SemaphoreType.DMA((block_rows // 128,)),
            pltpu.VMEM(out, F32),
        ]
    return pl.pallas_call(
        functools.partial(attend_kernel, blocks, block_rows, first, last, scale, len(packed)),
        out_shape=jax.ShapeDtypeStruct(out, F32),
        in_specs=[VMEM] * len(args),
        out_specs=HBM if last else VMEM,
        scratch_shapes=scratch,
        compiler_params=pltpu.CompilerParams(vmem_limit_bytes=36 * MIB),
        cost_estimate=pl.CostEstimate(
            flops=rows * keys * cost, bytes_accessed=10**6, transcendentals=0
        ),
        name="attend",
    )(*args)


def ring_moves():
    every = [(y, z, c) for y in range(2) for z in range(8) for c in range(2)]
    at = lambda y, z, c: y * 16 + (z % 8) * 2 + c

    def along_z(step):
        return [(at(y, z, c), at(y, z + (step if c == 0 else -step), c)) for y, z, c in every]

    across = [(at(y, z, c), at(1 - y, z, c)) for y, z, c in every]
    other = [(at(y, z, c), at(y, z, 1 - c)) for y, z, c in every]
    return along_z, across, other


def shards(
    features,
    conv_gain,
    conv_weight,
    conv_bias,
    tower_gain,
    query_weight,
    key_weight,
    value_weight,
    out_gain,
):
    count = lax.axis_size("seq")
    before = lax.ppermute(features[-2:], "seq", [(i, i + 1) for i in range(count - 1)])
    after = lax.ppermute(features[:2], "seq", [(i + 1, i) for i in range(count - 1)])
    gain = conv_gain.reshape(1, -1)
    taps = activate(features, gain)
    halo = jnp.concatenate([before, after], axis=0)
    normed = convolve(
        taps, halo, gain, conv_weight, conv_bias.reshape(1, -1), tower_gain.reshape(1, -1)
    )
    own = pack_keys_values(normed, key_weight, value_weight)
    along_z, across, other = ring_moves()
    z = lambda block, step: lax.ppermute(block, "seq", along_z(step))
    y = lambda block: lax.ppermute(block, "seq", across)
    c = lambda block: lax.ppermute(block, "seq", other)
    hold = lax.optimization_barrier
    block_rows = normed.shape[0]
    scale = math.log2(math.e) / math.sqrt(key_weight.shape[1])
    own_c = c(own)
    cat = lambda *blocks: jnp.concatenate(blocks, axis=0)
    chip = cat(own, own_c)
    z2 = z(chip, 2)
    z1 = z(chip, 1)
    y0 = y(own)
    queries = project_queries(normed, query_weight)
    part = functools.partial(attend, block_rows=block_rows, scale=scale)
    acc = part([own, own_c], queries, None, cost=640)
    y0, acc = hold((y0, acc))
    y0_c = c(y0)
    yz1 = z(cat(y0, y0_c), 1)
    acc = part([y0, y0_c], queries, acc, cost=640)
    z2, acc = hold((z2, acc))
    half_z2 = z2[: own.shape[0]]
    z4 = z(half_z2, 2)
    z3 = z(z2, 1)
    y2 = y(z2)
    z2_c = c(z2)
    z1, z2_c, acc = hold((z1, z2_c, acc))
    z1_c = c(z1)
    acc = part([z2, z2_c, z1], queries, acc, cost=640)
    z1_c, z3, acc = hold((z1_c, z3, acc))
    y3 = y(z3)
    acc = part([z1_c], queries, acc, cost=6400)
    z4, y2, acc = hold((z4, y2, acc))
    y4 = y(z4)
    near = cat(z3, z4, y2, yz1)
    near_c = c(near)
    acc = part([near], queries, acc, cost=6400)
    acc = part([near_c], queries, acc, cost=6400)
    y3, y4, acc = hold((y3, y4, acc))
    last = cat(y3, y4)
    last_c = c(last)
    acc = part([last], queries, acc, cost=6400)
    return part([last_c], queries, acc, out_gain=out_gain)


def solution(mesh):
    placed = (P(("dp", "seq"), None), P(), P(), P(), P(), P(), P(), P(), P())
    return jax.shard_map(
        shards, mesh=mesh, in_specs=placed, out_specs=P(("dp", "seq"), None), check_vma=False
    )
```

```python
import functools
import math

import jax
import jax.numpy as jnp
from jax import lax
from jax.experimental import pallas as pl
from jax.experimental.pallas import tpu as pltpu
from jax.sharding import PartitionSpec as P

F32 = jnp.float32
BF16 = jnp.bfloat16
EPS = 1e-06
MIB = 2**20
CONV_LIMIT = 47
ACT_LIMIT = 47
SHIFT = 32.0
BIG = 2.0**100
VMEM = pl.BlockSpec(memory_space=pltpu.VMEM)
HBM = pl.BlockSpec(memory_space=pltpu.HBM)


def norm_gelu(rows, gain):
    mean_sq = jnp.mean(rows * rows, axis=-1, keepdims=True)
    normed = rows * lax.rsqrt(mean_sq + EPS) * gain
    return 0.5 * normed * (1.0 + lax.erf(normed * math.sqrt(0.5)))


PHASES = ((0, 1), (1, 2), (2, 3), (3, 5))


def activate_kernel(feat_ref, gain_ref, weight_ref, taps_ref, lead_ref, scr, sem):
    rows, cin = feat_ref.shape
    lead = pltpu.make_async_copy(weight_ref.at[0], lead_ref, sem)
    lead.start()
    half = rows // 2
    active = norm_gelu(feat_ref[...].astype(F32), gain_ref[...])
    place = lax.broadcasted_iota(jnp.int32, (half, 128), 0)
    for i in range(cin // 128):
        scr[i] = active[:, i * 128 : (i + 1) * 128]
        even = scr[i, pl.ds(0, half, stride=2), :]
        odd = scr[i, pl.ds(1, half, stride=2), :]
        taps = [
            jnp.where(place == 0, 0.0, pltpu.roll(even, 1, 0)),
            jnp.where(place == 0, 0.0, pltpu.roll(odd, 1, 0)),
            even,
            odd,
            jnp.where(place == half - 1, 0.0, pltpu.roll(even, half - 1, 0)),
            jnp.where(place == half - 1, 0.0, pltpu.roll(odd, half - 1, 0)),
        ]
        for j, tap in enumerate(taps):
            at = j * cin + i * 128
            taps_ref[:, at : at + 128] = tap.astype(BF16)
    lead.wait()


def activate(features, gain, weight):
    rows, cin = features.shape
    return pl.pallas_call(
        activate_kernel,
        out_shape=(
            jax.ShapeDtypeStruct((rows // 2, 6 * cin), BF16),
            jax.ShapeDtypeStruct(weight.shape[1:], BF16),
        ),
        in_specs=[VMEM, VMEM, HBM],
        out_specs=(VMEM, VMEM),
        scratch_shapes=[pltpu.VMEM((cin // 128, rows, 128), F32), pltpu.SemaphoreType.DMA],
        compiler_params=pltpu.CompilerParams(vmem_limit_bytes=ACT_LIMIT * MIB),
        cost_estimate=pl.CostEstimate(flops=10**9, bytes_accessed=10**6, transcendentals=0),
        name="activate",
    )(features, gain, weight)


def conv_kernel(
    taps_ref,
    lead_ref,
    halo_ref,
    gain_ref,
    weight_ref,
    bias_ref,
    tower_ref,
    normed_ref,
    rows_scr,
    weight_scr,
    sums_scr,
    pooled_scr,
    sems,
):
    taps_n, cin, depth = weight_ref.shape
    half = taps_ref.shape[0]
    chunk = 256
    steps = depth // chunk

    def fetch(tap):
        return pltpu.make_async_copy(
            weight_ref.at[tap], weight_scr.at[pl.ds((tap - 1) * cin, cin), :], sems.at[tap - 1]
        )

    for tap in range(1, taps_n):
        fetch(tap).start()

    rows_scr[:half] = taps_ref[:, : taps_n * cin]
    rows_scr[half:] = taps_ref[:, cin:]
    halo = norm_gelu(halo_ref[...].astype(F32), gain_ref[...])
    lead = lax.broadcasted_iota(jnp.int32, (16, cin), 0)

    def put(row, at, col, value):
        old = rows_scr[at : at + 16, col : col + cin].astype(F32)
        rows_scr[at : at + 16, col : col + cin] = jnp.where(lead == row, value, old).astype(BF16)

    put(0, 0, 0, halo[0:1])
    put(0, 0, cin, halo[1:2])
    put(0, half, 0, halo[1:2])
    put(15, half - 16, 4 * cin, halo[2:3])
    put(15, 2 * half - 16, 3 * cin, halo[2:3])
    put(15, 2 * half - 16, 4 * cin, halo[3:4])

    square = jnp.zeros((half, 1), F32)
    for begin, end in PHASES:
        for tap in range(max(begin, 1), end):
            fetch(tap).wait()
        deep = slice(begin * cin, end * cin)
        held = slice((begin - 1) * cin, (end - 1) * cin)
        for step in range(steps):
            cols = slice(step * chunk, (step + 1) * chunk)
            weight = lead_ref[:, cols] if begin == 0 else weight_scr[held, cols]
            both = jnp.dot(rows_scr[:, deep], weight, preferred_element_type=F32)
            both = both + (bias_ref[:, cols] if begin == 0 else sums_scr[:, cols])
            if end < taps_n:
                sums_scr[:, cols] = both
            else:
                pooled = jnp.maximum(both[:half], both[half:]).astype(BF16)
                pooled_scr[:, cols] = pooled
                part = pooled.astype(F32)
                square = square + jnp.sum(part * part, axis=1, keepdims=True)
    factor = lax.rsqrt(square / depth + EPS)
    normed_ref[...] = (pooled_scr[...].astype(F32) * factor * tower_ref[...]).astype(BF16)


def convolve(taps, lead, halo, conv_gain, weight, bias, tower_gain):
    half = taps.shape[0]
    taps_n, cin, depth = weight.shape
    return pl.pallas_call(
        conv_kernel,
        out_shape=jax.ShapeDtypeStruct((half, depth), BF16),
        in_specs=[VMEM, VMEM, VMEM, VMEM, HBM, VMEM, VMEM],
        out_specs=VMEM,
        scratch_shapes=[
            pltpu.VMEM((2 * half, taps_n * cin), BF16),
            pltpu.VMEM(((taps_n - 1) * cin, depth), BF16),
            pltpu.VMEM((2 * half, depth), F32),
            pltpu.VMEM((half, depth), BF16),
            pltpu.SemaphoreType.DMA((taps_n - 1,)),
        ],
        compiler_params=pltpu.CompilerParams(vmem_limit_bytes=CONV_LIMIT * MIB),
        cost_estimate=pl.CostEstimate(flops=5 * 10**9, bytes_accessed=10**7, transcendentals=0),
        name="convolve",
    )(taps, lead, halo, conv_gain, weight, bias, tower_gain)


def pack_kernel(normed_ref, key_ref, value_ref, packed_ref):
    half = normed_ref.shape[0]
    normed = normed_ref[...]
    packed_ref[:half] = jnp.dot(normed, key_ref[...], preferred_element_type=F32).astype(BF16)
    values = lax.dot_general(
        normed, value_ref[...], (((1,), (1,)), ((), ())), preferred_element_type=F32
    )
    packed_ref[half : 2 * half] = values[:, :128].astype(BF16)
    rest = values[:, 128:]
    packed_ref[2 * half :] = jnp.concatenate(
        [rest[: half // 2], rest[half // 2 :]], axis=1
    ).astype(BF16)


def pack_keys_values(normed, key_weight, value_weight):
    return pl.pallas_call(
        pack_kernel,
        out_shape=jax.ShapeDtypeStruct((normed.shape[0] * 5 // 2, 128), BF16),
        in_specs=[VMEM] * 3,
        out_specs=VMEM,
        compiler_params=pltpu.CompilerParams(vmem_limit_bytes=8 * MIB),
        cost_estimate=pl.CostEstimate(flops=2 * 10**8, bytes_accessed=10**6, transcendentals=0),
        name="pack",
    )(normed, key_weight, value_weight.T)


def query_kernel(normed_ref, weight_ref, out_ref):
    rows = normed_ref.shape[0]
    chunk = 256
    for at in range(0, weight_ref.shape[1], chunk):
        result = jnp.dot(
            normed_ref[...], weight_ref[:, at : at + chunk], preferred_element_type=F32
        ).astype(BF16)
        for col in range(0, chunk, 128):
            head = (at + col) // 128
            out_ref[head * rows : (head + 1) * rows] = result[:, col : col + 128]


def project_queries(normed, weight):
    rows = normed.shape[0]
    return pl.pallas_call(
        query_kernel,
        out_shape=jax.ShapeDtypeStruct((weight.shape[1] // 128 * rows, 128), BF16),
        in_specs=[VMEM, VMEM],
        out_specs=VMEM,
        compiler_params=pltpu.CompilerParams(vmem_limit_bytes=16 * MIB),
        cost_estimate=pl.CostEstimate(flops=8 * 10**8, bytes_accessed=4 * 10**6, transcendentals=0),
        name="queries",
    )(normed, weight)


def attend_kernel(blocks, block_rows, first, last, scale, n_in, *refs):
    packed = refs[:n_in]
    q_ref = refs[n_in]
    rest = list(refs[n_in + 1 :])
    acc_ref = None if first else rest.pop(0)
    gain_ref = rest.pop(0) if last else None
    out_ref, probs, keys, vals = rest.pop(0), rest.pop(0), rest.pop(0), rest.pop(0)
    sums = rest.pop(0) if last else out_ref
    rows = q_ref.shape[0]
    tile = probs.shape[0]
    width = block_rows * 5 // 2
    ones = jnp.ones((block_rows // 2, 64), BF16)
    at = 0
    for ref in packed:
        for base in range(0, ref.shape[0], width):
            mid, end = at + block_rows // 2, at + block_rows
            keys[at:end] = ref[base : base + block_rows, :]
            vals[at:end, :128] = ref[base + block_rows : base + 2 * block_rows, :]
            tail = ref[base + 2 * block_rows : base + width, :]
            vals[at:mid, 128:] = jnp.concatenate([tail[:, :64], ones], axis=1)
            vals[mid:end, 128:] = jnp.concatenate([tail[:, 64:], ones], axis=1)
            at = end

    def scores(q, at):
        part = lax.dot_general(
            q, keys[at, :], (((1,), (1,)), ((), ())), preferred_element_type=F32
        )
        return part * scale

    def weigh(q, shift):
        for j in range(blocks):
            at = slice(j * block_rows, (j + 1) * block_rows)
            probs[:, at] = jnp.exp2(scores(q, at) - shift).astype(BF16)
        return jnp.dot(probs[...], vals[...], preferred_element_type=F32)

    def one_tile(t, worst):
        at = slice(t * tile, (t + 1) * tile)
        q = q_ref[at, :]
        if first:
            top = jnp.max(scores(q, slice(0, block_rows)), axis=1, keepdims=True)
            shift = jnp.broadcast_to(top + SHIFT, (tile, 128))
        else:
            shift = acc_ref[at, 256:]
        new = weigh(q, jnp.concatenate([shift] * (block_rows // 128), axis=1))
        if not first:
            new = new + acc_ref[at, :256]
        sums[at, :256] = new
        sums[at, 256:] = shift
        return jnp.maximum(worst, jnp.where(new[:, 128:] <= BIG, 0.0, 1.0))

    worst = jnp.zeros((tile, 128), F32)
    for t in range(rows // tile):
        worst = one_tile(t, worst)

    def redo(t, _):
        at = pl.ds(pl.multiple_of(t * 128, 128), 128)
        q = q_ref[at, :]

        def block(j):
            return pl.ds(pl.multiple_of(j * block_rows, block_rows), block_rows)

        def higher(j, top):
            return jnp.maximum(top, jnp.max(scores(q, block(j)), axis=1, keepdims=True) + SHIFT)

        old = jnp.full((128, 1), -jnp.inf, F32) if first else acc_ref[at, 256:257]
        top = lax.fori_loop(0, blocks, higher, old)

        def add(j, total):
            part = jnp.exp2(scores(q, block(j)) - top).astype(BF16)
            return total + jnp.dot(part, vals[block(j), :], preferred_element_type=F32)

        start = jnp.zeros((128, 256), F32) if first else acc_ref[at, :256] * jnp.exp2(old - top)
        total = lax.fori_loop(0, blocks, add, start)
        sums[at, :256] = total
        sums[at, 256:] = jnp.broadcast_to(top, (128, 128))
        return 0

    @pl.when(jnp.max(worst) > 0.0)
    def _():
        lax.fori_loop(0, rows // 128, redo, 0)

    if last:
        heads = rows // block_rows
        step = 128
        sem = rest.pop(0)
        stage = rest.pop(0)
        square = jnp.zeros((block_rows, 1), F32)
        inverse = []
        for h in range(heads):
            at = slice(h * block_rows, (h + 1) * block_rows)
            part = sums[at, :192]
            inverse.append(1.0 / sums[at, 192:193])
            size = jnp.sum(part * part, axis=1, keepdims=True)
            square = square + size * inverse[h] * inverse[h]
        factor = lax.rsqrt(square / (heads * 192) + EPS)
        inverse = [i * factor for i in inverse]
        copies = []
        for r in range(0, block_rows, step):
            for h in range(0, heads, 2):
                pair = [
                    sums[i * block_rows + r : i * block_rows + r + step, :192]
                    * inverse[i][r : r + step]
                    for i in (h, h + 1)
                ]
                cols = slice(h * 192, (h + 2) * 192)
                stage[r : r + step, cols] = jnp.concatenate(pair, axis=1) * gain_ref[:, cols]
            copies.append(
                pltpu.make_async_copy(
                    stage.at[pl.ds(r, step)], out_ref.at[pl.ds(r, step)], sem.at[r // step]
                )
            )
            copies[-1].start()
        for copy in copies:
            copy.wait()


def attend(packed, queries, acc, *, block_rows, scale, out_gain=None, cost=640):
    first, last = acc is None, out_gain is not None
    width = block_rows * 5 // 2
    blocks = sum(p.shape[0] for p in packed) // width
    rows = queries.shape[0]
    tile = 1024
    args = list(packed) + [queries]
    if not first:
        args.append(acc)
    if last:
        args.append(out_gain.reshape(1, -1))
    out = (block_rows, rows // block_rows * 192) if last else (rows, 384)
    keys = blocks * block_rows
    scratch = [
        pltpu.VMEM((tile, keys), BF16),
        pltpu.VMEM((keys, 128), BF16),
        pltpu.VMEM((keys, 256), BF16),
    ]
    if last:
        scratch += [
            pltpu.VMEM((rows, 384), F32),
            pltpu.SemaphoreType.DMA((block_rows // 128,)),
            pltpu.VMEM(out, F32),
        ]
    return pl.pallas_call(
        functools.partial(attend_kernel, blocks, block_rows, first, last, scale, len(packed)),
        out_shape=jax.ShapeDtypeStruct(out, F32),
        in_specs=[VMEM] * len(args),
        out_specs=HBM if last else VMEM,
        scratch_shapes=scratch,
        compiler_params=pltpu.CompilerParams(vmem_limit_bytes=36 * MIB),
        cost_estimate=pl.CostEstimate(
            flops=rows * keys * cost, bytes_accessed=10**6, transcendentals=0
        ),
        name="attend",
    )(*args)


def ring_moves():
    every = [(y, z, c) for y in range(2) for z in range(8) for c in range(2)]
    at = lambda y, z, c: y * 16 + (z % 8) * 2 + c

    def along_z(step):
        return [(at(y, z, c), at(y, z + (step if c == 0 else -step), c)) for y, z, c in every]

    across = [(at(y, z, c), at(1 - y, z, c)) for y, z, c in every]
    other = [(at(y, z, c), at(y, z, 1 - c)) for y, z, c in every]
    return along_z, across, other


def shards(
    features,
    conv_gain,
    conv_weight,
    conv_bias,
    tower_gain,
    query_weight,
    key_weight,
    value_weight,
    out_gain,
):
    count = lax.axis_size("seq")
    before = lax.ppermute(features[-2:], "seq", [(i, i + 1) for i in range(count - 1)])
    after = lax.ppermute(features[:2], "seq", [(i + 1, i) for i in range(count - 1)])
    gain = conv_gain.reshape(1, -1)
    taps, lead = activate(features, gain, conv_weight)
    halo = jnp.concatenate([before, after], axis=0)
    normed = convolve(
        taps, lead, halo, gain, conv_weight, conv_bias.reshape(1, -1), tower_gain.reshape(1, -1)
    )
    own = pack_keys_values(normed, key_weight, value_weight)
    along_z, across, other = ring_moves()
    z = lambda block, step: lax.ppermute(block, "seq", along_z(step))
    y = lambda block: lax.ppermute(block, "seq", across)
    c = lambda block: lax.ppermute(block, "seq", other)
    hold = lax.optimization_barrier
    block_rows = normed.shape[0]
    scale = math.log2(math.e) / math.sqrt(key_weight.shape[1])
    own_c = c(own)
    cat = lambda *blocks: jnp.concatenate(blocks, axis=0)
    chip = cat(own, own_c)
    z2 = z(chip, 2)
    z1 = z(chip, 1)
    y0 = y(own)
    queries = project_queries(normed, query_weight)
    part = functools.partial(attend, block_rows=block_rows, scale=scale)
    acc = part([own, own_c], queries, None, cost=640)
    y0, acc = hold((y0, acc))
    y0_c = c(y0)
    yz1 = z(cat(y0, y0_c), 1)
    acc = part([y0, y0_c], queries, acc, cost=640)
    z2, acc = hold((z2, acc))
    half_z2 = z2[: own.shape[0]]
    z4 = z(half_z2, 2)
    z3 = z(z2, 1)
    y2 = y(z2)
    z2_c = c(z2)
    z1, z2_c, acc = hold((z1, z2_c, acc))
    z1_c = c(z1)
    acc = part([z2, z2_c, z1], queries, acc, cost=640)
    z1_c, z3, acc = hold((z1_c, z3, acc))
    y3 = y(z3)
    acc = part([z1_c], queries, acc, cost=6400)
    z4, y2, acc = hold((z4, y2, acc))
    y4 = y(z4)
    near = cat(z3, z4, y2, yz1)
    near_c = c(near)
    acc = part([near], queries, acc, cost=6400)
    acc = part([near_c], queries, acc, cost=6400)
    y3, y4, acc = hold((y3, y4, acc))
    last = cat(y3, y4)
    last_c = c(last)
    acc = part([last], queries, acc, cost=6400)
    return part([last_c], queries, acc, out_gain=out_gain)


def solution(mesh):
    placed = (P(("dp", "seq"), None), P(), P(), P(), P(), P(), P(), P(), P())
    return jax.shard_map(
        shards, mesh=mesh, in_specs=placed, out_specs=P(("dp", "seq"), None), check_vma=False
    )
```

```python
import functools
import math

import jax
import jax.numpy as jnp
from jax import lax
from jax.experimental import pallas as pl
from jax.experimental.pallas import tpu as pltpu
from jax.sharding import PartitionSpec as P

F32 = jnp.float32
BF16 = jnp.bfloat16
EPS = 1e-06
MIB = 2**20
CONV_LIMIT = 47
ACT_LIMIT = 47
SHIFT = 32.0
BIG = 2.0**100
VMEM = pl.BlockSpec(memory_space=pltpu.VMEM)
HBM = pl.BlockSpec(memory_space=pltpu.HBM)


def norm_gelu(rows, gain):
    mean_sq = jnp.mean(rows * rows, axis=-1, keepdims=True)
    normed = rows * lax.rsqrt(mean_sq + EPS) * gain
    return 0.5 * normed * (1.0 + lax.erf(normed * math.sqrt(0.5)))


PHASES = ((0, 1), (1, 2), (2, 3), (3, 5))


def activate_kernel(feat_ref, gain_ref, weight_ref, taps_ref, lead_ref, scr, sem):
    rows, cin = feat_ref.shape
    lead = pltpu.make_async_copy(weight_ref.at[0], lead_ref, sem)
    lead.start()
    half = rows // 2
    active = norm_gelu(feat_ref[...].astype(F32), gain_ref[...])
    place = lax.broadcasted_iota(jnp.int32, (half, 128), 0)
    for i in range(cin // 128):
        scr[i] = active[:, i * 128 : (i + 1) * 128]
        even = scr[i, pl.ds(0, half, stride=2), :]
        odd = scr[i, pl.ds(1, half, stride=2), :]
        taps = [
            jnp.where(place == 0, 0.0, pltpu.roll(even, 1, 0)),
            jnp.where(place == 0, 0.0, pltpu.roll(odd, 1, 0)),
            even,
            odd,
            jnp.where(place == half - 1, 0.0, pltpu.roll(even, half - 1, 0)),
            jnp.where(place == half - 1, 0.0, pltpu.roll(odd, half - 1, 0)),
        ]
        for j, tap in enumerate(taps):
            at = j * cin + i * 128
            taps_ref[:, at : at + 128] = tap.astype(BF16)
    lead.wait()


def activate(features, gain, weight):
    rows, cin = features.shape
    return pl.pallas_call(
        activate_kernel,
        out_shape=(
            jax.ShapeDtypeStruct((rows // 2, 6 * cin), BF16),
            jax.ShapeDtypeStruct(weight.shape[1:], BF16),
        ),
        in_specs=[VMEM, VMEM, HBM],
        out_specs=(VMEM, VMEM),
        scratch_shapes=[pltpu.VMEM((cin // 128, rows, 128), F32), pltpu.SemaphoreType.DMA],
        compiler_params=pltpu.CompilerParams(vmem_limit_bytes=ACT_LIMIT * MIB),
        cost_estimate=pl.CostEstimate(flops=10**9, bytes_accessed=10**6, transcendentals=0),
        name="activate",
    )(features, gain, weight)


def conv_kernel(
    taps_ref,
    lead_ref,
    halo_ref,
    gain_ref,
    weight_ref,
    bias_ref,
    tower_ref,
    normed_ref,
    rows_scr,
    weight_scr,
    sums_scr,
    pooled_scr,
    sems,
):
    taps_n, cin, depth = weight_ref.shape
    half = taps_ref.shape[0]
    chunk = 256
    steps = depth // chunk

    def fetch(tap):
        return pltpu.make_async_copy(
            weight_ref.at[tap], weight_scr.at[pl.ds((tap - 1) * cin, cin), :], sems.at[tap - 1]
        )

    for tap in (1, 2):
        fetch(tap).start()

    rows_scr[:half] = taps_ref[:, : taps_n * cin]
    rows_scr[half:] = taps_ref[:, cin:]
    halo = norm_gelu(halo_ref[...].astype(F32), gain_ref[...])
    lead = lax.broadcasted_iota(jnp.int32, (16, cin), 0)

    def put(row, at, col, value):
        old = rows_scr[at : at + 16, col : col + cin].astype(F32)
        rows_scr[at : at + 16, col : col + cin] = jnp.where(lead == row, value, old).astype(BF16)

    put(0, 0, 0, halo[0:1])
    put(0, 0, cin, halo[1:2])
    put(0, half, 0, halo[1:2])
    put(15, half - 16, 4 * cin, halo[2:3])
    put(15, 2 * half - 16, 3 * cin, halo[2:3])
    put(15, 2 * half - 16, 4 * cin, halo[3:4])

    square = jnp.zeros((half, 1), F32)
    for begin, end in PHASES:
        for tap in range(max(begin, 1), end):
            fetch(tap).wait()
            if tap + 2 < taps_n:
                fetch(tap + 2).start()
        deep = slice(begin * cin, end * cin)
        held = slice((begin - 1) * cin, (end - 1) * cin)
        for step in range(steps):
            cols = slice(step * chunk, (step + 1) * chunk)
            weight = lead_ref[:, cols] if begin == 0 else weight_scr[held, cols]
            both = jnp.dot(rows_scr[:, deep], weight, preferred_element_type=F32)
            both = both + (bias_ref[:, cols] if begin == 0 else sums_scr[:, cols])
            if end < taps_n:
                sums_scr[:, cols] = both
            else:
                pooled = jnp.maximum(both[:half], both[half:]).astype(BF16)
                pooled_scr[:, cols] = pooled
                part = pooled.astype(F32)
                square = square + jnp.sum(part * part, axis=1, keepdims=True)
    factor = lax.rsqrt(square / depth + EPS)
    normed_ref[...] = (pooled_scr[...].astype(F32) * factor * tower_ref[...]).astype(BF16)


def convolve(taps, lead, halo, conv_gain, weight, bias, tower_gain):
    half = taps.shape[0]
    taps_n, cin, depth = weight.shape
    return pl.pallas_call(
        conv_kernel,
        out_shape=jax.ShapeDtypeStruct((half, depth), BF16),
        in_specs=[VMEM, VMEM, VMEM, VMEM, HBM, VMEM, VMEM],
        out_specs=VMEM,
        scratch_shapes=[
            pltpu.VMEM((2 * half, taps_n * cin), BF16),
            pltpu.VMEM(((taps_n - 1) * cin, depth), BF16),
            pltpu.VMEM((2 * half, depth), F32),
            pltpu.VMEM((half, depth), BF16),
            pltpu.SemaphoreType.DMA((taps_n - 1,)),
        ],
        compiler_params=pltpu.CompilerParams(vmem_limit_bytes=CONV_LIMIT * MIB),
        cost_estimate=pl.CostEstimate(flops=5 * 10**9, bytes_accessed=10**7, transcendentals=0),
        name="convolve",
    )(taps, lead, halo, conv_gain, weight, bias, tower_gain)


def pack_kernel(normed_ref, key_ref, value_ref, packed_ref):
    half = normed_ref.shape[0]
    normed = normed_ref[...]
    packed_ref[:half] = jnp.dot(normed, key_ref[...], preferred_element_type=F32).astype(BF16)
    values = lax.dot_general(
        normed, value_ref[...], (((1,), (1,)), ((), ())), preferred_element_type=F32
    )
    packed_ref[half : 2 * half] = values[:, :128].astype(BF16)
    rest = values[:, 128:]
    packed_ref[2 * half :] = jnp.concatenate(
        [rest[: half // 2], rest[half // 2 :]], axis=1
    ).astype(BF16)


def pack_keys_values(normed, key_weight, value_weight):
    return pl.pallas_call(
        pack_kernel,
        out_shape=jax.ShapeDtypeStruct((normed.shape[0] * 5 // 2, 128), BF16),
        in_specs=[VMEM] * 3,
        out_specs=VMEM,
        compiler_params=pltpu.CompilerParams(vmem_limit_bytes=8 * MIB),
        cost_estimate=pl.CostEstimate(flops=2 * 10**8, bytes_accessed=10**6, transcendentals=0),
        name="pack",
    )(normed, key_weight, value_weight.T)


def query_kernel(normed_ref, weight_ref, out_ref):
    rows = normed_ref.shape[0]
    chunk = 256
    for at in range(0, weight_ref.shape[1], chunk):
        result = jnp.dot(
            normed_ref[...], weight_ref[:, at : at + chunk], preferred_element_type=F32
        ).astype(BF16)
        for col in range(0, chunk, 128):
            head = (at + col) // 128
            out_ref[head * rows : (head + 1) * rows] = result[:, col : col + 128]


def project_queries(normed, weight):
    rows = normed.shape[0]
    return pl.pallas_call(
        query_kernel,
        out_shape=jax.ShapeDtypeStruct((weight.shape[1] // 128 * rows, 128), BF16),
        in_specs=[VMEM, VMEM],
        out_specs=VMEM,
        compiler_params=pltpu.CompilerParams(vmem_limit_bytes=16 * MIB),
        cost_estimate=pl.CostEstimate(flops=8 * 10**8, bytes_accessed=4 * 10**6, transcendentals=0),
        name="queries",
    )(normed, weight)


def attend_kernel(blocks, block_rows, first, last, scale, n_in, *refs):
    packed = refs[:n_in]
    q_ref = refs[n_in]
    rest = list(refs[n_in + 1 :])
    acc_ref = None if first else rest.pop(0)
    gain_ref = rest.pop(0) if last else None
    out_ref, probs, keys, vals = rest.pop(0), rest.pop(0), rest.pop(0), rest.pop(0)
    sums = rest.pop(0) if last else out_ref
    rows = q_ref.shape[0]
    tile = probs.shape[0]
    width = block_rows * 5 // 2
    ones = jnp.ones((block_rows // 2, 64), BF16)
    at = 0
    for ref in packed:
        for base in range(0, ref.shape[0], width):
            mid, end = at + block_rows // 2, at + block_rows
            keys[at:end] = ref[base : base + block_rows, :]
            vals[at:end, :128] = ref[base + block_rows : base + 2 * block_rows, :]
            tail = ref[base + 2 * block_rows : base + width, :]
            vals[at:mid, 128:] = jnp.concatenate([tail[:, :64], ones], axis=1)
            vals[mid:end, 128:] = jnp.concatenate([tail[:, 64:], ones], axis=1)
            at = end

    def scores(q, at):
        part = lax.dot_general(
            q, keys[at, :], (((1,), (1,)), ((), ())), preferred_element_type=F32
        )
        return part * scale

    def weigh(q, shift):
        for j in range(blocks):
            at = slice(j * block_rows, (j + 1) * block_rows)
            probs[:, at] = jnp.exp2(scores(q, at) - shift).astype(BF16)
        return jnp.dot(probs[...], vals[...], preferred_element_type=F32)

    def one_tile(t, worst):
        at = slice(t * tile, (t + 1) * tile)
        q = q_ref[at, :]
        if first:
            top = jnp.max(scores(q, slice(0, block_rows)), axis=1, keepdims=True)
            shift = jnp.broadcast_to(top + SHIFT, (tile, 128))
        else:
            shift = acc_ref[at, 256:]
        new = weigh(q, jnp.concatenate([shift] * (block_rows // 128), axis=1))
        if not first:
            new = new + acc_ref[at, :256]
        sums[at, :256] = new
        sums[at, 256:] = shift
        return jnp.maximum(worst, jnp.where(new[:, 128:] <= BIG, 0.0, 1.0))

    worst = jnp.zeros((tile, 128), F32)
    for t in range(rows // tile):
        worst = one_tile(t, worst)

    def redo(t, _):
        at = pl.ds(pl.multiple_of(t * 128, 128), 128)
        q = q_ref[at, :]

        def block(j):
            return pl.ds(pl.multiple_of(j * block_rows, block_rows), block_rows)

        def higher(j, top):
            return jnp.maximum(top, jnp.max(scores(q, block(j)), axis=1, keepdims=True) + SHIFT)

        old = jnp.full((128, 1), -jnp.inf, F32) if first else acc_ref[at, 256:257]
        top = lax.fori_loop(0, blocks, higher, old)

        def add(j, total):
            part = jnp.exp2(scores(q, block(j)) - top).astype(BF16)
            return total + jnp.dot(part, vals[block(j), :], preferred_element_type=F32)

        start = jnp.zeros((128, 256), F32) if first else acc_ref[at, :256] * jnp.exp2(old - top)
        total = lax.fori_loop(0, blocks, add, start)
        sums[at, :256] = total
        sums[at, 256:] = jnp.broadcast_to(top, (128, 128))
        return 0

    @pl.when(jnp.max(worst) > 0.0)
    def _():
        lax.fori_loop(0, rows // 128, redo, 0)

    if last:
        heads = rows // block_rows
        step = 128
        sem = rest.pop(0)
        stage = rest.pop(0)
        square = jnp.zeros((block_rows, 1), F32)
        inverse = []
        for h in range(heads):
            at = slice(h * block_rows, (h + 1) * block_rows)
            part = sums[at, :192]
            inverse.append(1.0 / sums[at, 192:193])
            size = jnp.sum(part * part, axis=1, keepdims=True)
            square = square + size * inverse[h] * inverse[h]
        factor = lax.rsqrt(square / (heads * 192) + EPS)
        inverse = [i * factor for i in inverse]
        copies = []
        for r in range(0, block_rows, step):
            for h in range(0, heads, 2):
                pair = [
                    sums[i * block_rows + r : i * block_rows + r + step, :192]
                    * inverse[i][r : r + step]
                    for i in (h, h + 1)
                ]
                cols = slice(h * 192, (h + 2) * 192)
                stage[r : r + step, cols] = jnp.concatenate(pair, axis=1) * gain_ref[:, cols]
            copies.append(
                pltpu.make_async_copy(
                    stage.at[pl.ds(r, step)], out_ref.at[pl.ds(r, step)], sem.at[r // step]
                )
            )
            copies[-1].start()
        for copy in copies:
            copy.wait()


def attend(packed, queries, acc, *, block_rows, scale, out_gain=None, cost=640):
    first, last = acc is None, out_gain is not None
    width = block_rows * 5 // 2
    blocks = sum(p.shape[0] for p in packed) // width
    rows = queries.shape[0]
    tile = 1024
    args = list(packed) + [queries]
    if not first:
        args.append(acc)
    if last:
        args.append(out_gain.reshape(1, -1))
    out = (block_rows, rows // block_rows * 192) if last else (rows, 384)
    keys = blocks * block_rows
    scratch = [
        pltpu.VMEM((tile, keys), BF16),
        pltpu.VMEM((keys, 128), BF16),
        pltpu.VMEM((keys, 256), BF16),
    ]
    if last:
        scratch += [
            pltpu.VMEM((rows, 384), F32),
            pltpu.SemaphoreType.DMA((block_rows // 128,)),
            pltpu.VMEM(out, F32),
        ]
    return pl.pallas_call(
        functools.partial(attend_kernel, blocks, block_rows, first, last, scale, len(packed)),
        out_shape=jax.ShapeDtypeStruct(out, F32),
        in_specs=[VMEM] * len(args),
        out_specs=HBM if last else VMEM,
        scratch_shapes=scratch,
        compiler_params=pltpu.CompilerParams(vmem_limit_bytes=36 * MIB),
        cost_estimate=pl.CostEstimate(
            flops=rows * keys * cost, bytes_accessed=10**6, transcendentals=0
        ),
        name="attend",
    )(*args)


def ring_moves():
    every = [(y, z, c) for y in range(2) for z in range(8) for c in range(2)]
    at = lambda y, z, c: y * 16 + (z % 8) * 2 + c

    def along_z(step):
        return [(at(y, z, c), at(y, z + (step if c == 0 else -step), c)) for y, z, c in every]

    across = [(at(y, z, c), at(1 - y, z, c)) for y, z, c in every]
    other = [(at(y, z, c), at(y, z, 1 - c)) for y, z, c in every]
    return along_z, across, other


def shards(
    features,
    conv_gain,
    conv_weight,
    conv_bias,
    tower_gain,
    query_weight,
    key_weight,
    value_weight,
    out_gain,
):
    count = lax.axis_size("seq")
    before = lax.ppermute(features[-2:], "seq", [(i, i + 1) for i in range(count - 1)])
    after = lax.ppermute(features[:2], "seq", [(i + 1, i) for i in range(count - 1)])
    gain = conv_gain.reshape(1, -1)
    taps, lead = activate(features, gain, conv_weight)
    halo = jnp.concatenate([before, after], axis=0)
    normed = convolve(
        taps, lead, halo, gain, conv_weight, conv_bias.reshape(1, -1), tower_gain.reshape(1, -1)
    )
    own = pack_keys_values(normed, key_weight, value_weight)
    along_z, across, other = ring_moves()
    z = lambda block, step: lax.ppermute(block, "seq", along_z(step))
    y = lambda block: lax.ppermute(block, "seq", across)
    c = lambda block: lax.ppermute(block, "seq", other)
    hold = lax.optimization_barrier
    block_rows = normed.shape[0]
    scale = math.log2(math.e) / math.sqrt(key_weight.shape[1])
    own_c = c(own)
    cat = lambda *blocks: jnp.concatenate(blocks, axis=0)
    chip = cat(own, own_c)
    z2 = z(chip, 2)
    z1 = z(chip, 1)
    y0 = y(own)
    queries = project_queries(normed, query_weight)
    part = functools.partial(attend, block_rows=block_rows, scale=scale)
    acc = part([own, own_c], queries, None, cost=640)
    y0, acc = hold((y0, acc))
    y0_c = c(y0)
    yz1 = z(cat(y0, y0_c), 1)
    acc = part([y0, y0_c], queries, acc, cost=640)
    z2, acc = hold((z2, acc))
    half_z2 = z2[: own.shape[0]]
    z4 = z(half_z2, 2)
    z3 = z(z2, 1)
    y2 = y(z2)
    z2_c = c(z2)
    z1, z2_c, acc = hold((z1, z2_c, acc))
    z1_c = c(z1)
    acc = part([z2, z2_c, z1], queries, acc, cost=640)
    z1_c, z3, acc = hold((z1_c, z3, acc))
    y3 = y(z3)
    acc = part([z1_c], queries, acc, cost=6400)
    z4, y2, acc = hold((z4, y2, acc))
    y4 = y(z4)
    near = cat(z3, z4, y2, yz1)
    near_c = c(near)
    acc = part([near], queries, acc, cost=6400)
    acc = part([near_c], queries, acc, cost=6400)
    y3, y4, acc = hold((y3, y4, acc))
    last = cat(y3, y4)
    last_c = c(last)
    acc = part([last], queries, acc, cost=6400)
    return part([last_c], queries, acc, out_gain=out_gain)


def solution(mesh):
    placed = (P(("dp", "seq"), None), P(), P(), P(), P(), P(), P(), P(), P())
    return jax.shard_map(
        shards, mesh=mesh, in_specs=placed, out_specs=P(("dp", "seq"), None), check_vma=False
    )
```
